32 devices in a mesh: grp: 2 (over y), tm: 8 (over z, x), space: 2 (over core).
Axes of the slice: x: 2, y: 2, z: 4, core: 2. Of those that a mesh axis runs over, the one named last changes fastest.
Arguments:
- tokens: bfloat16 [16, 24, 64, 1024], P(('grp', 'tm'), 'space'), parts along dimension 0, may hold values from -28 to 28
- gains: float32 [2, 1024], replicated, may hold values from 0.5 to 2
- qkv_weights: bfloat16 [2, 1024, 1536], replicated, may hold values from -1.125 to 1.125
- out_weights: bfloat16 [2, 512, 1024], replicated, may hold values from -0.25 to 0.25
Outputs:
- video_out: bfloat16 [16, 24, 64, 1024], P(('grp', 'tm'), 'space'), parts along dimension 0
The draws below stay inside these ranges and needn't reach their ends.
There are 2 independent parts, one for each index of `grp`. The reference program is written for one: setup_inputs(seed, part) draws one part's arguments, and reference() takes and returns one part's arrays. A program takes and returns all parts, laid end to end along the dimension named above; an argument that names none is the same for every part. Nothing has to cross between parts.
All inputs are finite; a program needn't handle non-finite values.
Results may differ from the reference program's by a relative error of at most 0.007.
Values may be sent and summed in bfloat16 or wider, within the bound.
A program may use at most 64 MiB of HBM per device.

```python
import math
import jax
import jax.numpy as jnp
from jax import lax

D = 1024
HEADS = 8
HEAD = 64
COLS = 64
HEIGHT = 24
FRAMES = 8


def draw_tokens(key, part):
    full_shape = (FRAMES, HEIGHT, COLS, D)
    return jnp.clip(jax.random.normal(key, full_shape, jnp.float32), -6.0, 6.0).astype(jnp.bfloat16)


def draw_qkv_weights(key, part):
    inner_width = HEADS * HEAD
    full_shape = (2, D, 3 * inner_width)
    key_main = jax.random.fold_in(key, 0)
    matrix = jnp.clip(jax.random.normal(key_main, full_shape, jnp.float32), -6.0, 6.0) / math.sqrt(D)
    return matrix.astype(jnp.bfloat16)


def gaussian(key, shape, width, bound, held_as=jnp.bfloat16):
    entries = jax.random.normal(key, shape, jnp.float32) * width
    return jnp.minimum(jnp.maximum(entries, -bound), bound).astype(held_as)


def setup_inputs(seed: int = 0, part: int = 0) -> dict:
    splits = jax.random.split(jax.random.key(seed), 5)
    part_splits = jax.random.split(jax.random.fold_in(splits[4], part), 5)
    return {
        "tokens": draw_tokens(jax.random.fold_in(jax.random.fold_in(splits[4], part), 71), part),
        "gains": jnp.clip(jnp.exp(jax.random.uniform(splits[1], (2, D), jnp.float32, math.log(0.5), math.log(2.0))), 0.5, 2.0),
        "qkv_weights": draw_qkv_weights(jax.random.fold_in(splits[4], 71), part),
        "out_weights": gaussian(splits[3], (2, HEADS * HEAD, D), (HEADS * HEAD) ** -0.5, 0.25),
    }


def attend_groups(stream, gain_row, qkv_weight, out_weight):
    group_n, length, feat_count = stream.shape
    widened = stream.astype(jnp.float32)
    normed = (widened * lax.rsqrt(lax.optimization_barrier(jnp.mean(widened * widened, axis=-1, keepdims=True)) + 1e-06) * gain_row).astype(jnp.bfloat16)
    projected = jnp.dot(normed.reshape(group_n * length, feat_count), qkv_weight, preferred_element_type=jnp.float32).astype(jnp.bfloat16)
    shaped = projected.reshape(group_n, length, 3, HEADS, HEAD).astype(jnp.float32)
    scores = jnp.einsum('gqhd,gkhd->ghqk', shaped[:, :, 0], shaped[:, :, 1]) * HEAD ** (-0.5)
    row_max = lax.optimization_barrier(jnp.max(scores, axis=-1, keepdims=True))
    raised = jnp.exp(scores - row_max)
    weights = (raised / lax.optimization_barrier(jnp.sum(raised, axis=-1, keepdims=True))).astype(jnp.bfloat16)
    mixture = jnp.einsum('ghqk,gkhd->gqhd', weights.astype(jnp.float32), shaped[:, :, 2]).astype(jnp.bfloat16)
    mixture = mixture.reshape(group_n * length, HEADS * HEAD)
    update = jnp.dot(mixture, out_weight, preferred_element_type=jnp.float32).reshape(group_n, length, feat_count)
    return (widened + update).astype(jnp.bfloat16)

def reference(tokens, gains, qkv_weights, out_weights):
    frame_n, height_n, column_n, feat_count = tokens.shape
    by_column = jnp.transpose(tokens, (0, 2, 1, 3)).reshape(frame_n * column_n, height_n, feat_count)
    spatial = attend_groups(by_column, gains[0], qkv_weights[0], out_weights[0]).reshape(frame_n, column_n, height_n, feat_count)
    by_frame = jnp.transpose(spatial, (2, 1, 0, 3)).reshape(height_n * column_n, frame_n, feat_count)
    temporal = attend_groups(by_frame, gains[1], qkv_weights[1], out_weights[1]).reshape(height_n, column_n, frame_n, feat_count)
    return jnp.transpose(temporal, (2, 0, 1, 3))
```

```python
import functools

import jax
import jax.numpy as jnp
from jax import lax
from jax.experimental import pallas as pl
from jax.experimental.pallas import tpu as pltpu
from jax.sharding import PartitionSpec as P

HEADS = 8
HEAD = 64
WIDTH = 16
MESH = pl.DeviceIdType.MESH


def block_groups(groups, length):
    target = max(1, 512 // length)
    chosen = 1
    for candidate in range(1, min(groups, target) + 1):
        if groups % candidate == 0:
            chosen = candidate
    return chosen


def attend(tokens, length, gain_row, qkv_weight, out_weight):
    tok_count, feat_count = tokens.shape
    inner_width = out_weight.shape[0]
    stream = tokens.astype(jnp.float32)
    normed = (
        stream * lax.rsqrt(jnp.mean(stream * stream, axis=-1, keepdims=True) + 1e-06) * gain_row
    ).astype(jnp.bfloat16)
    projected = jnp.dot(normed, qkv_weight, preferred_element_type=jnp.float32).astype(jnp.bfloat16)
    per_block = block_groups(tok_count // length, length) * length
    blocks = tok_count // per_block
    shaped = projected.reshape(blocks, per_block, 3, HEADS, HEAD)
    scores = jnp.einsum(
        "bqhd,bkhd->bhqk", shaped[:, :, 0], shaped[:, :, 1], preferred_element_type=jnp.float32
    ) * HEAD ** (-0.5)
    group_ids = jnp.arange(per_block) // length
    same_group = group_ids[:, None] == group_ids[None, :]
    scores = jnp.where(same_group, scores, -1e30)
    row_max = jnp.max(scores, axis=-1, keepdims=True)
    raised = jnp.exp(scores - row_max)
    weights = (raised / jnp.sum(raised, axis=-1, keepdims=True)).astype(jnp.bfloat16)
    mixture = jnp.einsum(
        "bhqk,bkhd->bqhd", weights, shaped[:, :, 2], preferred_element_type=jnp.float32
    ).astype(jnp.bfloat16)
    mixture = mixture.reshape(tok_count, inner_width)
    update = jnp.dot(mixture, out_weight, preferred_element_type=jnp.float32)
    return (stream + update).astype(jnp.bfloat16)


def shards(tokens, gains, qkv_weights, out_weights):
    spread = lax.axis_size("space")
    frame_count = lax.axis_size("tm")
    frame_tokens = tokens[0]
    row_count, col_count, feat_count = frame_tokens.shape
    half_cols = col_count // spread
    transposed = jnp.transpose(frame_tokens, (1, 0, 2)).reshape(
        spread, half_cols, row_count, feat_count
    )
    piece = lax.all_to_all(transposed, "space", split_axis=0, concat_axis=2, tiled=True)
    col_items = piece.shape[1]
    height_n = piece.shape[2]
    flat = piece.reshape(col_items * height_n, feat_count)
    done = attend(flat, height_n, gains[0], qkv_weights[0], out_weights[0])
    columns_done = done.reshape(1, col_items, height_n, feat_count)
    regrouped = columns_done.reshape(half_cols, spread, row_count, feat_count).transpose(0, 2, 1, 3)
    span = col_count * row_count // frame_count
    regrouped = regrouped.reshape(frame_count, span, 1, feat_count)
    piece = lax.all_to_all(regrouped, "tm", split_axis=0, concat_axis=2, tiled=True)
    pos_items = piece.shape[1]
    frame_n = piece.shape[2]
    flat = piece.reshape(pos_items * frame_n, feat_count)
    done = attend(flat, frame_n, gains[1], qkv_weights[1], out_weights[1])
    timed = done.reshape(1, pos_items, frame_n, feat_count)
    paired = timed.reshape(span // spread, spread, frame_count, feat_count).transpose(0, 2, 1, 3)
    paired = paired.reshape(span // spread, frame_count * spread, feat_count)
    back_rows = lax.all_to_all(paired, ("tm", "space"), split_axis=1, concat_axis=0, tiled=True)
    back_rows = back_rows.reshape(frame_count, spread, span // spread, feat_count).transpose(
        1, 0, 2, 3
    )
    restored = back_rows.reshape(col_count, row_count, feat_count)
    return jnp.transpose(restored, (1, 0, 2))[None]


def head_mix(q, k, v, width):
    rows, inner = q.shape
    keys = k.shape[0]
    lanes = 4 * HEAD
    shape = (width, keys)
    same = lax.broadcasted_iota(jnp.int32, shape, 0) == lax.rem(
        lax.broadcasted_iota(jnp.int32, shape, 1), width
    )
    bias = jnp.where(same, 0.0, -1e30)[None]
    lane = lax.broadcasted_iota(jnp.int32, (rows, lanes), 1) // HEAD
    parts = []
    for start in range(0, inner, lanes):
        q4 = q[:, start : start + lanes]
        stacked = jnp.concatenate(
            [jnp.where(lane == i, q4, jnp.zeros_like(q4)) for i in range(4)], axis=0
        )
        scores = lax.dot_general(
            stacked, k[:, start : start + lanes], (((1,), (1,)), ((), ())),
            preferred_element_type=jnp.float32,
        )
        scores = scores.reshape(4 * rows // width, width, keys) + bias
        raised = jnp.exp((scores - jnp.max(scores, axis=-1, keepdims=True)) * HEAD ** (-0.5))
        total = jnp.sum(raised, axis=-1, keepdims=True).reshape(4 * rows, 1)
        mixed = jnp.dot(
            raised.reshape(4 * rows, keys).astype(jnp.bfloat16), v[:, start : start + lanes],
            preferred_element_type=jnp.float32,
        ) / total
        out = mixed[:rows]
        for i in range(1, 4):
            out = jnp.where(lane == i, mixed[i * rows : (i + 1) * rows], out)
        parts.append(out.astype(jnp.bfloat16))
    return jnp.concatenate(parts, axis=1)


def norm(x, gain):
    wide = x.astype(jnp.float32)
    return (
        wide * lax.rsqrt(jnp.mean(wide * wide, axis=-1, keepdims=True) + 1e-06) * gain
    ).astype(jnp.bfloat16)


def dot(a, b):
    return jnp.dot(a, b, preferred_element_type=jnp.float32)


def kernel(
    n, tok_hbm, gain_ref, qkv_hbm, wo_hbm, out_hbm,
    x_vm, wqkv, wo, q_vm, kv, h_vm, h_in, mix, mix_in, out_vm,
    x_sem, w_sem, kv_send, kv_recv, h_send, h_recv, m_send, m_recv, o_sem,
):
    rows, groups, width, feat = tok_hbm.shape
    inner = wo.shape[1]
    slots = h_in.shape[0]
    blocks = rows * groups
    per = rows * width
    me = lax.axis_index("tm")
    other = 1 - lax.axis_index("space")

    def load_x(c):
        return pltpu.make_async_copy(tok_hbm.at[:, c], x_vm.at[c], x_sem.at[c])

    def load_w(i):
        if i % 2 == 0:
            return pltpu.make_async_copy(qkv_hbm.at[i // 2], wqkv.at[i // 2], w_sem.at[i])
        return pltpu.make_async_copy(wo_hbm.at[i // 2], wo.at[i // 2], w_sem.at[i])

    load_x(0).start()
    load_w(0).start()
    for c in range(1, groups):
        load_x(c).start()
    for i in range(1, 4):
        load_w(i).start()

    barrier = pltpu.get_barrier_semaphore()
    pl.semaphore_signal(barrier, inc=1, device_id={"space": other}, device_id_type=MESH)

    def greet(i, carry):
        to = lax.rem(me + i, n)
        pl.semaphore_signal(barrier, inc=1, device_id={"tm": to}, device_id_type=MESH)
        return carry

    lax.fori_loop(1, n, greet, 0)

    def send_kv(c):
        return pltpu.make_async_remote_copy(
            src_ref=kv.at[c, 0], dst_ref=kv.at[c, 1],
            send_sem=kv_send.at[c], recv_sem=kv_recv.at[c],
            device_id={"space": other}, device_id_type=MESH,
        )

    def project(c):
        load_x(c).wait()
        normed = norm(x_vm[c].reshape(per, feat), gain_ref[0:1, :])
        kv[c, 0] = dot(normed, wqkv[0, :, inner:]).astype(jnp.bfloat16)
        q_vm[c] = dot(normed, wqkv[0, :, :inner]).astype(jnp.bfloat16)

    load_w(0).wait()
    project(0)
    pl.semaphore_wait(barrier, n)
    send_kv(0).start()
    load_w(1).wait()

    def height(c, carry):
        @pl.when(c + 1 < groups)
        def _():
            project(c + 1)
            send_kv(c + 1).start()

        send_kv(c).wait()
        both = kv[c].reshape(2 * per, 2 * inner)
        mixture = head_mix(q_vm[c], both[:, :inner], both[:, inner:], width)
        x = x_vm[c].reshape(per, feat).astype(jnp.float32)
        done = (x + dot(mixture, wo[0])).astype(jnp.bfloat16)
        h_vm[pl.ds(c * rows, rows)] = done.reshape(rows, width, feat)

        def push(i, carry):
            b = c * rows + lax.rem(i + me, rows)
            to = lax.rem(b, n)
            s = lax.div(b, n)

            @pl.when(to == me)
            def _():
                pltpu.make_async_copy(h_vm.at[b], h_in.at[s, me], h_recv.at[s]).start()

            @pl.when(to != me)
            def _():
                pltpu.make_async_remote_copy(
                    src_ref=h_vm.at[b], dst_ref=h_in.at[s, me],
                    send_sem=h_send, recv_sem=h_recv.at[s],
                    device_id={"tm": to}, device_id_type=MESH,
                ).start()

            return carry

        return lax.fori_loop(0, rows, push, carry)

    lax.fori_loop(0, groups, height, 0)
    load_w(2).wait()

    def temporal(s, carry):
        pltpu.make_async_copy(h_in.at[s], h_in.at[s], h_recv.at[s]).wait()
        normed = norm(h_in[s].reshape(n * width, feat), gain_ref[1:2, :])
        kv_now = dot(normed, wqkv[1, :, inner:]).astype(jnp.bfloat16)
        q_now = dot(normed, wqkv[1, :, :inner]).astype(jnp.bfloat16)
        mixture = head_mix(q_now, kv_now[:, :inner], kv_now[:, inner:], width)
        mix[s] = mixture.reshape(n, width, inner)
        pltpu.make_async_copy(mix.at[s, me], mix_in.at[s, me], m_recv.at[s]).start()

        def push(i, carry):
            to = lax.rem(me + i, n)
            pltpu.make_async_remote_copy(
                src_ref=mix.at[s, to], dst_ref=mix_in.at[s, me],
                send_sem=m_send, recv_sem=m_recv.at[s],
                device_id={"tm": to}, device_id_type=MESH,
            ).start()
            return carry

        return lax.fori_loop(1, n, push, carry)

    lax.fori_loop(0, slots, temporal, 0)
    load_w(3).wait()

    def finish(s, carry):
        pltpu.make_async_copy(mix_in.at[s], mix_in.at[s], m_recv.at[s]).wait()
        update = dot(mix_in[s].reshape(n * width, inner), wo[1])
        h = h_vm[pl.ds(s * n, n)].reshape(n * width, feat).astype(jnp.float32)
        out_vm[pl.ds(s * n, n)] = (h + update).astype(jnp.bfloat16).reshape(n, width, feat)

        def store(i, carry):
            b = s * n + i
            pltpu.make_async_copy(
                out_vm.at[b], out_hbm.at[lax.rem(b, rows), lax.div(b, rows)], o_sem
            ).start()
            return carry

        return lax.fori_loop(0, n, store, carry)

    lax.fori_loop(0, slots, finish, 0)
    sent = slots * (n - 1)
    pltpu.make_async_copy(h_vm.at[pl.ds(0, sent)], h_vm.at[pl.ds(0, sent)], h_send).wait()
    pltpu.make_async_copy(
        out_vm.at[pl.ds(0, sent), :, pl.ds(0, inner)],
        out_vm.at[pl.ds(0, sent), :, pl.ds(0, inner)], m_send,
    ).wait()
    pltpu.make_async_copy(out_vm, out_vm, o_sem).wait()


def fused(tokens, gains, qkv_weights, out_weights):
    n = lax.axis_size("tm")
    _, rows, cols, feat = tokens.shape
    inner = out_weights.shape[1]
    groups = cols // WIDTH
    blocks = rows * groups
    slots = blocks // n
    per = rows * WIDTH
    bf16 = jnp.bfloat16
    out = pl.pallas_call(
        functools.partial(kernel, n),
        out_shape=jax.ShapeDtypeStruct((rows, groups, WIDTH, feat), bf16),
        in_specs=[
            pl.BlockSpec(memory_space=pl.ANY),
            pl.BlockSpec(memory_space=pltpu.VMEM),
            pl.BlockSpec(memory_space=pl.ANY),
            pl.BlockSpec(memory_space=pl.ANY),
        ],
        out_specs=pl.BlockSpec(memory_space=pl.ANY),
        scratch_shapes=[
            pltpu.VMEM((groups, rows, WIDTH, feat), bf16),
            pltpu.VMEM(qkv_weights.shape, bf16),
            pltpu.VMEM(out_weights.shape, bf16),
            pltpu.VMEM((groups, per, inner), bf16),
            pltpu.VMEM((groups, 2, per, 2 * inner), bf16),
            pltpu.VMEM((blocks, WIDTH, feat), bf16),
            pltpu.VMEM((slots, n, WIDTH, feat), bf16),
            pltpu.VMEM((slots, n, WIDTH, inner), bf16),
            pltpu.VMEM((slots, n, WIDTH, inner), bf16),
            pltpu.VMEM((blocks, WIDTH, feat), bf16),
            pltpu.SemaphoreType.DMA((groups,)),
            pltpu.SemaphoreType.DMA((4,)),
            pltpu.SemaphoreType.DMA((groups,)),
            pltpu.SemaphoreType.DMA((groups,)),
            pltpu.SemaphoreType.DMA,
            pltpu.SemaphoreType.DMA((slots,)),
            pltpu.SemaphoreType.DMA,
            pltpu.SemaphoreType.DMA((slots,)),
            pltpu.SemaphoreType.DMA,
        ],
        compiler_params=pltpu.CompilerParams(
            collective_id=0, has_side_effects=True, vmem_limit_bytes=50 * 2**20
        ),
    )(tokens.reshape(rows, groups, WIDTH, feat), gains, qkv_weights, out_weights)
    return out.reshape(tokens.shape)


def body(tokens, gains, qkv_weights, out_weights):
    n = lax.axis_size("tm")
    _, rows, cols, _ = tokens.shape
    fits = (
        lax.axis_size("space") == 2
        and cols % WIDTH == 0
        and (rows * (cols // WIDTH)) % n == 0
        and tokens.shape[0] == 1
    )
    plan = fused if fits else shards
    return plan(tokens, gains, qkv_weights, out_weights)


def solution(mesh):
    return jax.shard_map(
        body,
        mesh=mesh,
        in_specs=(P(("grp", "tm"), "space", None, None), P(), P(), P()),
        out_specs=P(("grp", "tm"), "space", None, None),
        check_vma=False,
    )
```

```python
import functools

import jax
import jax.numpy as jnp
from jax import lax
from jax.experimental import pallas as pl
from jax.experimental.pallas import tpu as pltpu
from jax.sharding import PartitionSpec as P

HEADS = 8
HEAD = 64
WIDTH = 16
MESH = pl.DeviceIdType.MESH


def block_groups(groups, length):
    target = max(1, 512 // length)
    chosen = 1
    for candidate in range(1, min(groups, target) + 1):
        if groups % candidate == 0:
            chosen = candidate
    return chosen


def attend(tokens, length, gain_row, qkv_weight, out_weight):
    tok_count, feat_count = tokens.shape
    inner_width = out_weight.shape[0]
    stream = tokens.astype(jnp.float32)
    normed = (
        stream * lax.rsqrt(jnp.mean(stream * stream, axis=-1, keepdims=True) + 1e-06) * gain_row
    ).astype(jnp.bfloat16)
    projected = jnp.dot(normed, qkv_weight, preferred_element_type=jnp.float32).astype(jnp.bfloat16)
    per_block = block_groups(tok_count // length, length) * length
    blocks = tok_count // per_block
    shaped = projected.reshape(blocks, per_block, 3, HEADS, HEAD)
    scores = jnp.einsum(
        "bqhd,bkhd->bhqk", shaped[:, :, 0], shaped[:, :, 1], preferred_element_type=jnp.float32
    ) * HEAD ** (-0.5)
    group_ids = jnp.arange(per_block) // length
    same_group = group_ids[:, None] == group_ids[None, :]
    scores = jnp.where(same_group, scores, -1e30)
    row_max = jnp.max(scores, axis=-1, keepdims=True)
    raised = jnp.exp(scores - row_max)
    weights = (raised / jnp.sum(raised, axis=-1, keepdims=True)).astype(jnp.bfloat16)
    mixture = jnp.einsum(
        "bhqk,bkhd->bqhd", weights, shaped[:, :, 2], preferred_element_type=jnp.float32
    ).astype(jnp.bfloat16)
    mixture = mixture.reshape(tok_count, inner_width)
    update = jnp.dot(mixture, out_weight, preferred_element_type=jnp.float32)
    return (stream + update).astype(jnp.bfloat16)


def shards(tokens, gains, qkv_weights, out_weights):
    spread = lax.axis_size("space")
    frame_count = lax.axis_size("tm")
    frame_tokens = tokens[0]
    row_count, col_count, feat_count = frame_tokens.shape
    half_cols = col_count // spread
    transposed = jnp.transpose(frame_tokens, (1, 0, 2)).reshape(
        spread, half_cols, row_count, feat_count
    )
    piece = lax.all_to_all(transposed, "space", split_axis=0, concat_axis=2, tiled=True)
    col_items = piece.shape[1]
    height_n = piece.shape[2]
    flat = piece.reshape(col_items * height_n, feat_count)
    done = attend(flat, height_n, gains[0], qkv_weights[0], out_weights[0])
    columns_done = done.reshape(1, col_items, height_n, feat_count)
    regrouped = columns_done.reshape(half_cols, spread, row_count, feat_count).transpose(0, 2, 1, 3)
    span = col_count * row_count // frame_count
    regrouped = regrouped.reshape(frame_count, span, 1, feat_count)
    piece = lax.all_to_all(regrouped, "tm", split_axis=0, concat_axis=2, tiled=True)
    pos_items = piece.shape[1]
    frame_n = piece.shape[2]
    flat = piece.reshape(pos_items * frame_n, feat_count)
    done = attend(flat, frame_n, gains[1], qkv_weights[1], out_weights[1])
    timed = done.reshape(1, pos_items, frame_n, feat_count)
    paired = timed.reshape(span // spread, spread, frame_count, feat_count).transpose(0, 2, 1, 3)
    paired = paired.reshape(span // spread, frame_count * spread, feat_count)
    back_rows = lax.all_to_all(paired, ("tm", "space"), split_axis=1, concat_axis=0, tiled=True)
    back_rows = back_rows.reshape(frame_count, spread, span // spread, feat_count).transpose(
        1, 0, 2, 3
    )
    restored = back_rows.reshape(col_count, row_count, feat_count)
    return jnp.transpose(restored, (1, 0, 2))[None]


def head_mix(q, k, v, width):
    rows, inner = q.shape
    keys = k.shape[0]
    lanes = 4 * HEAD
    shape = (width, keys)
    same = lax.broadcasted_iota(jnp.int32, shape, 0) == lax.rem(
        lax.broadcasted_iota(jnp.int32, shape, 1), width
    )
    bias = jnp.where(same, 0.0, -1e30)[None]
    lane = lax.broadcasted_iota(jnp.int32, (rows, lanes), 1) // HEAD
    parts = []
    for start in range(0, inner, lanes):
        q4 = q[:, start : start + lanes]
        stacked = jnp.concatenate(
            [jnp.where(lane == i, q4, jnp.zeros_like(q4)) for i in range(4)], axis=0
        )
        scores = lax.dot_general(
            stacked, k[:, start : start + lanes], (((1,), (1,)), ((), ())),
            preferred_element_type=jnp.float32,
        )
        scores = scores.reshape(4 * rows // width, width, keys) + bias
        raised = jnp.exp((scores - jnp.max(scores, axis=-1, keepdims=True)) * HEAD ** (-0.5))
        total = jnp.sum(raised, axis=-1, keepdims=True).reshape(4 * rows, 1)
        mixed = jnp.dot(
            raised.reshape(4 * rows, keys).astype(jnp.bfloat16), v[:, start : start + lanes],
            preferred_element_type=jnp.float32,
        ) / total
        out = mixed[:rows]
        for i in range(1, 4):
            out = jnp.where(lane == i, mixed[i * rows : (i + 1) * rows], out)
        parts.append(out.astype(jnp.bfloat16))
    return jnp.concatenate(parts, axis=1)


def norm(x, gain):
    wide = x.astype(jnp.float32)
    return (
        wide * lax.rsqrt(jnp.mean(wide * wide, axis=-1, keepdims=True) + 1e-06) * gain
    ).astype(jnp.bfloat16)


def dot(a, b):
    return jnp.dot(a, b, preferred_element_type=jnp.float32)


def kernel(
    n, tok_hbm, gain_hbm, qkv_hbm, wo_hbm, out_hbm,
    gain_ref, x_vm, wqkv, wo, q_vm, kv, h_vm, h_in, mix, mix_in, out_vm,
    gain_sem, x_sem, w_sem, kv_send, kv_recv, h_send, h_recv, m_send, m_recv, o_sem,
    early, early_in, e_send, e_recv,
):
    rows, groups, width, feat = tok_hbm.shape
    inner = wo.shape[1]
    slots = h_in.shape[0]
    blocks = rows * groups
    per = rows * width
    me = lax.axis_index("tm")
    other = 1 - lax.axis_index("space")

    def load_x(c):
        return pltpu.make_async_copy(tok_hbm.at[:, c], x_vm.at[c], x_sem.at[c])

    def load_w(i):
        if i % 2 == 0:
            return pltpu.make_async_copy(qkv_hbm.at[i // 2], wqkv.at[i // 2], w_sem.at[i])
        return pltpu.make_async_copy(wo_hbm.at[i // 2], wo.at[i // 2], w_sem.at[i])

    load_gain = pltpu.make_async_copy(gain_hbm, gain_ref, gain_sem)
    load_x(0).start()
    load_gain.start()
    load_w(0).start()
    for c in range(1, groups):
        load_x(c).start()
    for i in range(1, 4):
        load_w(i).start()

    barrier = pltpu.get_barrier_semaphore()
    pl.semaphore_signal(barrier, inc=1, device_id={"space": other}, device_id_type=MESH)

    def greet(i, carry):
        to = lax.rem(me + i, n)
        pl.semaphore_signal(barrier, inc=1, device_id={"tm": to}, device_id_type=MESH)
        return carry

    lax.fori_loop(1, n, greet, 0)

    def send_kv(c):
        return pltpu.make_async_remote_copy(
            src_ref=kv.at[c, 0], dst_ref=kv.at[c, 1],
            send_sem=kv_send.at[c], recv_sem=kv_recv.at[c],
            device_id={"space": other}, device_id_type=MESH,
        )

    def ahead(a, b):
        return lax.rem(lax.div(a, 2) + lax.div(b, 2), 2) == 1

    def send_ahead(src, dst, send, recv, to):
        return pltpu.make_async_remote_copy(
            src_ref=src, dst_ref=dst, send_sem=send, recv_sem=recv,
            device_id={"tm": to}, device_id_type=MESH,
        )

    def project(c):
        normed = norm(x_vm[c].reshape(per, feat), gain_ref[0:1, :])
        kv[c, 0] = dot(normed, wqkv[0, :, inner:]).astype(jnp.bfloat16)
        q_vm[c] = dot(normed, wqkv[0, :, :inner]).astype(jnp.bfloat16)

    load_x(0).wait()
    load_gain.wait()
    load_w(0).wait()
    project(0)
    pl.semaphore_wait(barrier, n)
    send_kv(0).start()

    def push_ahead(i, carry):
        to = lax.rem(me + i, n)

        @pl.when(ahead(me, to))
        def _():
            send_ahead(x_vm.at[0, to], h_in.at[0, me], h_send, h_recv.at[0], to).start()

        return carry

    lax.fori_loop(1, n, push_ahead, 0)
    load_w(1).wait()

    def height(c, carry):
        @pl.when(c + 1 < groups)
        def _():
            load_x(c + 1).wait()
            project(c + 1)
            send_kv(c + 1).start()

        send_kv(c).wait()
        both = kv[c].reshape(2 * per, 2 * inner)
        mixture = head_mix(q_vm[c], both[:, :inner], both[:, inner:], width)

        @pl.when(c == 0)
        def _():
            early[...] = mixture.reshape(rows, width, inner)

        x = x_vm[c].reshape(per, feat).astype(jnp.float32)
        done = (x + dot(mixture, wo[0])).astype(jnp.bfloat16)
        h_vm[pl.ds(c * rows, rows)] = done.reshape(rows, width, feat)

        def push(i, carry):
            b = c * rows + lax.rem(i + me, rows)
            to = lax.rem(b, n)
            s = lax.div(b, n)

            @pl.when(to == me)
            def _():
                pltpu.make_async_copy(h_vm.at[b], h_in.at[s, me], h_recv.at[s]).start()

            first = jnp.logical_and(s == 0, ahead(me, to))

            @pl.when(first)
            def _():
                send_ahead(early.at[to], early_in.at[me], e_send, e_recv, to).start()

            @pl.when(jnp.logical_and(to != me, jnp.logical_not(first)))
            def _():
                pltpu.make_async_remote_copy(
                    src_ref=h_vm.at[b], dst_ref=h_in.at[s, me],
                    send_sem=h_send, recv_sem=h_recv.at[s],
                    device_id={"tm": to}, device_id_type=MESH,
                ).start()

            return carry

        return lax.fori_loop(0, rows, push, carry)

    lax.fori_loop(0, groups, height, 0)
    load_w(2).wait()

    def temporal(s, carry):
        pltpu.make_async_copy(h_in.at[s], h_in.at[s], h_recv.at[s]).wait()

        @pl.when(s == 0)
        def _():
            half = early_in.at[pl.ds(0, n // 2)]
            pltpu.make_async_copy(half, half, e_recv).wait()
            update = dot(early_in[...].reshape(n * width, inner), wo[0])
            frame = lax.broadcasted_iota(jnp.int32, update.shape, 0) // width
            h = h_in[0].reshape(n * width, feat).astype(jnp.float32)
            h = h + jnp.where(ahead(frame, me), update, 0.0)
            h_in[0] = h.astype(jnp.bfloat16).reshape(n, width, feat)

        normed = norm(h_in[s].reshape(n * width, feat), gain_ref[1:2, :])
        kv_now = dot(normed, wqkv[1, :, inner:]).astype(jnp.bfloat16)
        q_now = dot(normed, wqkv[1, :, :inner]).astype(jnp.bfloat16)
        mixture = head_mix(q_now, kv_now[:, :inner], kv_now[:, inner:], width)
        mix[s] = mixture.reshape(n, width, inner)
        pltpu.make_async_copy(mix.at[s, me], mix_in.at[s, me], m_recv.at[s]).start()

        def push(i, carry):
            to = lax.rem(me + i, n)
            pltpu.make_async_remote_copy(
                src_ref=mix.at[s, to], dst_ref=mix_in.at[s, me],
                send_sem=m_send, recv_sem=m_recv.at[s],
                device_id={"tm": to}, device_id_type=MESH,
            ).start()
            return carry

        return lax.fori_loop(1, n, push, carry)

    lax.fori_loop(0, slots, temporal, 0)
    load_w(3).wait()

    def finish(s, carry):
        pltpu.make_async_copy(mix_in.at[s], mix_in.at[s], m_recv.at[s]).wait()
        update = dot(mix_in[s].reshape(n * width, inner), wo[1])
        h = h_vm[pl.ds(s * n, n)].reshape(n * width, feat).astype(jnp.float32)
        out_vm[pl.ds(s * n, n)] = (h + update).astype(jnp.bfloat16).reshape(n, width, feat)

        def store(i, carry):
            b = s * n + i
            pltpu.make_async_copy(
                out_vm.at[b], out_hbm.at[lax.rem(b, rows), lax.div(b, rows)], o_sem
            ).start()
            return carry

        return lax.fori_loop(0, n, store, carry)

    lax.fori_loop(0, slots, finish, 0)
    sent = slots * (n - 1)
    pltpu.make_async_copy(h_vm.at[pl.ds(0, sent)], h_vm.at[pl.ds(0, sent)], h_send).wait()
    pltpu.make_async_copy(
        out_vm.at[pl.ds(0, sent), :, pl.ds(0, inner)],
        out_vm.at[pl.ds(0, sent), :, pl.ds(0, inner)], m_send,
    ).wait()
    half = early.at[pl.ds(0, n // 2)]
    pltpu.make_async_copy(half, half, e_send).wait()
    pltpu.make_async_copy(out_vm, out_vm, o_sem).wait()


def fused(tokens, gains, qkv_weights, out_weights):
    n = lax.axis_size("tm")
    _, rows, cols, feat = tokens.shape
    inner = out_weights.shape[1]
    groups = cols // WIDTH
    blocks = rows * groups
    slots = blocks // n
    per = rows * WIDTH
    bf16 = jnp.bfloat16
    out = pl.pallas_call(
        functools.partial(kernel, n),
        out_shape=jax.ShapeDtypeStruct((rows, groups, WIDTH, feat), bf16),
        in_specs=[
            pl.BlockSpec(memory_space=pltpu.HBM),
            pl.BlockSpec(memory_space=pltpu.HBM),
            pl.BlockSpec(memory_space=pltpu.HBM),
            pl.BlockSpec(memory_space=pltpu.HBM),
        ],
        out_specs=pl.BlockSpec(memory_space=pl.ANY),
        scratch_shapes=[
            pltpu.VMEM(gains.shape, jnp.float32),
            pltpu.VMEM((groups, rows, WIDTH, feat), bf16),
            pltpu.VMEM(qkv_weights.shape, bf16),
            pltpu.VMEM(out_weights.shape, bf16),
            pltpu.VMEM((groups, per, inner), bf16),
            pltpu.VMEM((groups, 2, per, 2 * inner), bf16),
            pltpu.VMEM((blocks, WIDTH, feat), bf16),
            pltpu.VMEM((slots, n, WIDTH, feat), bf16),
            pltpu.VMEM((slots, n, WIDTH, inner), bf16),
            pltpu.VMEM((slots, n, WIDTH, inner), bf16),
            pltpu.VMEM((blocks, WIDTH, feat), bf16),
            pltpu.SemaphoreType.DMA,
            pltpu.SemaphoreType.DMA((groups,)),
            pltpu.SemaphoreType.DMA((4,)),
            pltpu.SemaphoreType.DMA((groups,)),
            pltpu.SemaphoreType.DMA((groups,)),
            pltpu.SemaphoreType.DMA,
            pltpu.SemaphoreType.DMA((slots,)),
            pltpu.SemaphoreType.DMA,
            pltpu.SemaphoreType.DMA((slots,)),
            pltpu.SemaphoreType.DMA,
            pltpu.VMEM((rows, WIDTH, inner), bf16),
            pltpu.VMEM((n, WIDTH, inner), bf16),
            pltpu.SemaphoreType.DMA,
            pltpu.SemaphoreType.DMA,
        ],
        compiler_params=pltpu.CompilerParams(
            collective_id=0, has_side_effects=True, vmem_limit_bytes=50 * 2**20
        ),
    )(tokens.reshape(rows, groups, WIDTH, feat), gains, qkv_weights, out_weights)
    return out.reshape(tokens.shape)


def body(tokens, gains, qkv_weights, out_weights):
    n = lax.axis_size("tm")
    _, rows, cols, _ = tokens.shape
    fits = (
        lax.axis_size("space") == 2
        and cols % WIDTH == 0
        and (rows * (cols // WIDTH)) % n == 0
        and tokens.shape[0] == 1
        and n % 4 == 0
        and n <= rows
    )
    plan = fused if fits else shards
    return plan(tokens, gains, qkv_weights, out_weights)


def solution(mesh):
    return jax.shard_map(
        body,
        mesh=mesh,
        in_specs=(P(("grp", "tm"), "space", None, None), P(), P(), P()),
        out_specs=P(("grp", "tm"), "space", None, None),
        check_vma=False,
    )
```
